32 devices in a mesh: sib: 2 (over core), row: 4 (over y, x), col: 4 (over z).
Axes of the slice: x: 2, y: 2, z: 4, core: 2. Of those that a mesh axis runs over, the one named last changes fastest.
Arguments:
- child_update: bfloat16 [2, 8192, 8192], P('sib', 'row', 'col'), may hold values from -6 to 6
- ext_map: int32 [2, 8192], replicated, may hold values from 0 to 16383, as said below
- diag_inverse: bfloat16 [2, 256, 256], replicated, as said below
Outputs:
- front_out: bfloat16 [16384, 16384], P('row', ('sib', 'col'))
- panel_out: bfloat16 [16384, 512], P('row')
The draws below stay inside these ranges and needn't reach their ends.
Inputs may be any that keep to these rules, and one draw needn't show every extreme that they name: For each child s, the 8192 values of ext_map[s] are distinct. For each child, the rows of one block of 2048 consecutive child rows land at most 512 times in each group of 2048 consecutive front rows and at most 1024 times in each block of 4096 front rows; both bounds are met in every draw. For each child, every block of 4096 front rows receives exactly 2048 child rows, every group of 2048 exactly half of that. Each diag_inverse[p] is lower triangular with positive diagonal.
All inputs are finite; a program needn't handle non-finite values.
Results may differ from the reference program's by a relative error of at most 0.0064.
Values may be sent and summed in bfloat16 or wider, within the bound.
A program may use at most 256 MiB of HBM per device.

```python
import math
import jax
import jax.numpy as jnp
from jax import lax

FRONT = 16384
CHILD = 8192
PANEL = 256
NPANEL = 2
CHILD_BLOCK = 2048
GROUPS = 8
FRONT_GROUP = 2048
MEAN_LOAD = 256


def child_rows_map(key, sibling):
    sub_key = jax.random.fold_in(key, 7919 + sibling)
    keys = jax.random.split(sub_key, 5)
    half = GROUPS // 2
    blocks_count = CHILD // CHILD_BLOCK
    mean_load = MEAN_LOAD
    half_load = mean_load // 2
    index_j = jnp.arange(half, dtype=jnp.int32)
    bumps = jax.random.randint(keys[0], (half, 2), 0, max(half_load, 1))
    pair_id = jnp.clip((index_j - 3) // 2, 0, half - 1)
    signs = jnp.where(index_j >= 3, jnp.where((index_j - 3) % 2 == 0, jnp.where(index_j + 1 < half, 1, 0), -1), 0)
    bump_rows = bumps[pair_id]
    loads = jnp.where(index_j[:, None] == 0, 2 * mean_load, jnp.where(index_j[:, None] < 3, half_load, mean_load + signs[:, None] * bump_rows))
    perm_groups = jax.random.permutation(keys[1], half)
    perm_blocks = jax.random.permutation(keys[2], blocks_count)
    which = (perm_groups[None, :] + perm_blocks[:, None]) % half
    counts = loads[which].reshape(blocks_count, GROUPS).astype(jnp.int32)
    group_before = jnp.cumsum(counts, axis=0) - counts
    block_before = jnp.cumsum(counts, axis=1) - counts
    shuffles = jax.vmap(lambda item: jax.random.permutation(item, CHILD_BLOCK))(jax.random.split(keys[3], blocks_count)).astype(jnp.int32)
    group_of = jnp.sum((block_before[:, None, :] <= shuffles[:, :, None]).astype(jnp.int32), axis=2) - 1
    inner = shuffles - jnp.take_along_axis(block_before, group_of, axis=1)
    place = jnp.take_along_axis(group_before, group_of, axis=1) + inner
    group_perm = jax.vmap(lambda item: jax.random.permutation(item, FRONT_GROUP))(jax.random.split(keys[4], GROUPS)).astype(jnp.int32)
    parent = group_of * FRONT_GROUP + group_perm[group_of, place]
    return parent.reshape(CHILD).astype(jnp.int32)


def draw_ext_map(key, part):
    return jnp.stack([child_rows_map(key, 0), child_rows_map(key, 1)]).astype(jnp.int32)


def draw_diag_inverse(key, part):
    keys = jax.random.split(jax.random.fold_in(key, 4243), 2)
    shape = (NPANEL, PANEL, PANEL)
    row_ids = lax.broadcasted_iota(jnp.int32, shape, 1)
    col_ids = lax.broadcasted_iota(jnp.int32, shape, 2)
    noise = jax.random.normal(keys[0], shape, jnp.float32)
    diag_scale = jax.random.uniform(keys[1], shape, jnp.float32, 0.1, 0.25)
    values = jnp.where(row_ids == col_ids, diag_scale, jnp.where(col_ids < row_ids, 0.2 * noise / math.sqrt(PANEL), 0.0))
    return values.astype(jnp.bfloat16)


def level_of(stream_key, extent, cuts, low, top_value):
    def one(position, parts):
        heights = jax.random.uniform(jax.random.fold_in(jax.random.fold_in(stream_key, 6), position), (parts,), jnp.float32, low / len(cuts), top_value / len(cuts))
        return jnp.repeat(jnp.exp(heights), extent[position] // parts).reshape((-1,) + (1,) * (len(extent) - position - 1))

    factor_of = one(*cuts[0])
    for cut in cuts[1:]:
        factor_of = factor_of * one(*cut)
    return factor_of


def gaussian(own_key, dims, deviation, reach, shards=(), kind=jnp.bfloat16):
    values = deviation * jax.random.normal(own_key, dims, jnp.float32)
    if shards:
        values = values * level_of(own_key, dims, shards, -0.22, 0.18)
    return jnp.clip(values, -reach, reach).astype(kind)


def setup_inputs(seed: int = 0) -> dict:
    seeds = jax.random.split(jax.random.key(seed), 4)
    return {
        "child_update": gaussian(seeds[0], (2, CHILD, CHILD), 1.0, 6.0, ((0, 2), (1, 4), (2, 4))),
        "ext_map": draw_ext_map(jax.random.fold_in(seeds[3], 71), 0),
        "diag_inverse": draw_diag_inverse(jax.random.fold_in(seeds[3], 71), 0),
    }


def reference(child_update, ext_map, diag_inverse):
    front_block = jnp.zeros((FRONT, FRONT), jnp.float32)
    for sibling in range(2):
        targets = ext_map[sibling].astype(jnp.int32)
        placed = jnp.zeros((FRONT, CHILD), jnp.float32).at[targets].set(child_update[sibling].astype(jnp.float32))
        front_block = front_block.at[:, targets].add(placed)
    factors = []
    for panel_step in range(NPANEL):
        column = front_block[:, panel_step * PANEL:(panel_step + 1) * PANEL].astype(jnp.bfloat16)
        factor = jnp.dot(column, diag_inverse[panel_step].T, preferred_element_type=jnp.float32).astype(jnp.bfloat16)
        front_block = front_block - jnp.dot(factor, factor.T, preferred_element_type=jnp.float32)
        factors.append(factor)
    return front_block.astype(jnp.bfloat16), jnp.concatenate(factors, axis=1)
```

```python
import jax
import jax.numpy as jnp
from jax import lax
from jax.sharding import PartitionSpec as P

FRONT = 16384
PANEL = 256
NPANEL = 2


def broadcast(shard, axis, root):
    mine = lax.axis_index(axis) == root
    return lax.psum(jnp.where(mine, shard, jnp.zeros_like(shard)), axis)


CHUNKS = 2
LAST = (((1,), (1,)), ((), ()))
PLAIN = (((1,), (0,)), ((), ()))


def dot(a, b, dims):
    return lax.dot_general(a, b, dims, preferred_element_type=jnp.float32)


def child_tables(ext_map, part_count, stride, block_rows):
    target = ext_map // stride
    part_ids = jnp.arange(part_count, dtype=jnp.int32)
    onehot = (target[:, :, None] == part_ids[None, None, :]).astype(jnp.int32)
    before = jnp.cumsum(onehot, axis=1) - onehot
    global_rank = jnp.sum(before * onehot, axis=2)
    block_start = before[:, ::block_rows, :]
    starts = jnp.repeat(block_start, block_rows, axis=1)
    local_rank = global_rank - jnp.sum(starts * onehot, axis=2)
    counts = jnp.sum(onehot.reshape(2, -1, block_rows, part_count), axis=2)
    return target, global_rank, local_rank, block_start, counts


def own_slice(table, side_index, first_row, block_rows):
    picked = lax.dynamic_index_in_dim(table, side_index, 0, keepdims=False)
    return lax.dynamic_slice_in_dim(picked, first_row, block_rows, 0)


def at_place(count, place, value):
    here = jnp.arange(count, dtype=jnp.int32)[:, None] == place[None, :]
    return jnp.sum(jnp.where(here, value[None, :] + 1, 0), axis=1) - 1


def hot(count, index):
    return (jnp.arange(count, dtype=jnp.int32)[:, None] == index[None, :]).astype(jnp.bfloat16)


def on_device(child_update, ext_map, diag_inverse):
    rows_grid = lax.axis_size("row")
    cols_grid = lax.axis_size("col")
    groups = lax.axis_size("sib") * cols_grid
    side = lax.axis_index("sib")
    row_pos = lax.axis_index("row")
    col_pos = lax.axis_index("col")
    group_pos = side * cols_grid + col_pos
    update = child_update[0]
    block_rows = child_update.shape[1]
    child_total = ext_map.shape[1]
    front_rows = FRONT // rows_grid
    front_cols = FRONT // groups
    mean_load = block_rows // groups
    cap_cols = 2 * mean_load
    cap_rows = 4 * mean_load // CHUNKS
    held_count = block_rows // CHUNKS
    wide = NPANEL * PANEL
    block_ids = jnp.arange(child_total, dtype=jnp.int32) // block_rows
    row_target, row_global, row_local, row_start, row_counts = child_tables(
        ext_map, rows_grid, front_rows, block_rows
    )
    col_target, _, col_local, _, _ = child_tables(ext_map, groups, front_cols, block_rows)

    own_target = own_slice(row_target, side, row_pos * block_rows, block_rows)
    own_local = own_slice(row_local, side, row_pos * block_rows, block_rows)
    own_global = own_slice(row_global, side, row_pos * block_rows, block_rows)
    own_slot = own_target * cap_rows + own_local // CHUNKS
    row_hot = [
        hot(rows_grid * cap_rows, jnp.where(own_global % CHUNKS == part, own_slot, -1))
        for part in range(CHUNKS)
    ]

    start_here = lax.dynamic_slice_in_dim(
        lax.dynamic_index_in_dim(row_start, side, 0, keepdims=False), row_pos, 1, 1
    )
    count_here = lax.dynamic_slice_in_dim(
        lax.dynamic_index_in_dim(row_counts, side, 0, keepdims=False), row_pos, 1, 1
    )
    slot_ids = jnp.arange(cap_rows, dtype=jnp.int32)[None, :] * CHUNKS
    pack_hot = []
    for part in range(CHUNKS):
        inner = slot_ids + (part - start_here) % CHUNKS
        packed = jnp.where(inner < count_here, (start_here + inner) // CHUNKS, -1)
        pack_hot.append(hot(held_count, packed.reshape(-1)))

    own_cext = own_slice(ext_map, side, col_pos * block_rows, block_rows)
    own_ctarget = own_slice(col_target, side, col_pos * block_rows, block_rows)
    own_crank = own_slice(col_local, side, col_pos * block_rows, block_rows)
    col_hot = hot(groups * cap_cols, own_ctarget * cap_cols + own_crank)

    def exchange(sent, width):
        arrived = lax.all_to_all(
            sent.reshape(rows_grid, cap_rows, width), "row", split_axis=0, concat_axis=0, tiled=True
        )
        return arrived.reshape(rows_grid * cap_rows, width)

    landed = []
    for part in range(CHUNKS):
        sent = dot(row_hot[part], update, PLAIN).astype(jnp.bfloat16)
        arrived = exchange(sent, block_rows)
        held = dot(pack_hot[part], arrived, PLAIN).astype(jnp.bfloat16)
        send_cols = dot(col_hot, held, LAST).astype(jnp.bfloat16)
        got = lax.all_to_all(
            send_cols.reshape(groups, cap_cols, held_count),
            ("sib", "col"),
            split_axis=0,
            concat_axis=0,
            tiled=True,
        )
        landed.append(got.reshape(2, cols_grid * cap_cols, held_count))

    row_place = []
    col_place = []
    for sibling in range(2):
        here = row_target[sibling] == row_pos
        order = (row_global[sibling] % CHUNKS) * held_count + row_global[sibling] // CHUNKS
        row_place.append(
            at_place(
                block_rows,
                jnp.where(here, order, -1),
                ext_map[sibling] - row_pos * front_rows,
            )
        )
        here = col_target[sibling] == group_pos
        col_place.append(
            at_place(
                cols_grid * cap_cols,
                jnp.where(here, block_ids * cap_cols + col_local[sibling], -1),
                ext_map[sibling] - group_pos * front_cols,
            )
        )

    strip = dot(update, hot(wide, own_cext), LAST).astype(jnp.bfloat16)
    strip = lax.psum(strip, "col")
    strips = []
    for part in range(CHUNKS):
        sent = dot(row_hot[part], strip, PLAIN).astype(jnp.bfloat16)
        strips.append(dot(pack_hot[part], exchange(sent, wide), PLAIN).astype(jnp.bfloat16))
    strip = jnp.concatenate(strips, axis=0)
    other = lax.ppermute(strip, "sib", [(0, 1), (1, 0)])
    own_rows = hot(front_rows, jnp.where(side == 0, row_place[0], row_place[1]))
    other_rows = hot(front_rows, jnp.where(side == 0, row_place[1], row_place[0]))
    panels = dot(own_rows, strip, PLAIN) + dot(other_rows, other, PLAIN)

    factors = []
    for step in range(NPANEL):
        column = panels[:, step * PANEL : (step + 1) * PANEL]
        for earlier, factor in enumerate(factors):
            first = step * PANEL
            top = lax.slice_in_dim(factor, first % front_rows, first % front_rows + PANEL, axis=0)
            top = broadcast(top, "row", first // front_rows)
            column = column - dot(factor, top, LAST)
        factors.append(dot(column.astype(jnp.bfloat16), diag_inverse[step], LAST).astype(jnp.bfloat16))
    factor = jnp.concatenate(factors, axis=1)
    root_row = group_pos * front_cols // front_rows
    start_row = group_pos * front_cols % front_rows
    across = broadcast(lax.dynamic_slice_in_dim(factor, start_row, front_cols, 0), "row", root_row)

    col_pick = [hot(front_cols, place) for place in col_place]
    front_block = -dot(factor, across, LAST)
    for part in range(CHUNKS):
        spread = jnp.concatenate(
            [dot(landed[part][s], col_pick[s], (((0,), (1,)), ((), ()))).astype(jnp.bfloat16) for s in range(2)],
            axis=0,
        )
        places = jnp.concatenate(
            [row_place[s][part * held_count : (part + 1) * held_count] for s in range(2)]
        )
        front_block = front_block + dot(hot(front_rows, places), spread, PLAIN)
    return front_block.astype(jnp.bfloat16), factor


def solution(mesh):
    placed = (P("sib", "row", "col"), P(), P())
    return jax.shard_map(
        on_device,
        mesh=mesh,
        in_specs=placed,
        out_specs=(P("row", ("sib", "col")), P("row", None)),
        check_vma=False,
    )
```

```python
import jax
import jax.numpy as jnp
from jax import lax
from jax.sharding import PartitionSpec as P

FRONT = 16384
PANEL = 256
NPANEL = 2


def broadcast(shard, axis, root):
    mine = lax.axis_index(axis) == root
    return lax.psum(jnp.where(mine, shard, jnp.zeros_like(shard)), axis)


CHUNKS = 2
LAST = (((1,), (1,)), ((), ()))
PLAIN = (((1,), (0,)), ((), ()))


def dot(a, b, dims):
    return lax.dot_general(a, b, dims, preferred_element_type=jnp.float32)


def child_tables(ext_map, part_count, stride, block_rows):
    target = ext_map // stride
    part_ids = jnp.arange(part_count, dtype=jnp.int32)
    onehot = (target[:, :, None] == part_ids[None, None, :]).astype(jnp.int32)
    before = jnp.cumsum(onehot, axis=1) - onehot
    global_rank = jnp.sum(before * onehot, axis=2)
    block_start = before[:, ::block_rows, :]
    starts = jnp.repeat(block_start, block_rows, axis=1)
    local_rank = global_rank - jnp.sum(starts * onehot, axis=2)
    counts = jnp.sum(onehot.reshape(2, -1, block_rows, part_count), axis=2)
    return target, global_rank, local_rank, block_start, counts


def own_slice(table, side_index, first_row, block_rows):
    picked = lax.dynamic_index_in_dim(table, side_index, 0, keepdims=False)
    return lax.dynamic_slice_in_dim(picked, first_row, block_rows, 0)


def at_place(count, place, value):
    here = jnp.arange(count, dtype=jnp.int32)[:, None] == place[None, :]
    return jnp.sum(jnp.where(here, value[None, :] + 1, 0), axis=1) - 1


def hot(count, index):
    return (jnp.arange(count, dtype=jnp.int32)[:, None] == index[None, :]).astype(jnp.bfloat16)


def on_device(child_update, ext_map, diag_inverse):
    rows_grid = lax.axis_size("row")
    cols_grid = lax.axis_size("col")
    groups = lax.axis_size("sib") * cols_grid
    side = lax.axis_index("sib")
    row_pos = lax.axis_index("row")
    col_pos = lax.axis_index("col")
    group_pos = side * cols_grid + col_pos
    update = child_update[0]
    block_rows = child_update.shape[1]
    child_total = ext_map.shape[1]
    front_rows = FRONT // rows_grid
    front_cols = FRONT // groups
    mean_load = block_rows // groups
    cap_cols = 2 * mean_load
    cap_rows = 4 * mean_load // CHUNKS
    held_count = block_rows // CHUNKS
    wide = NPANEL * PANEL
    block_ids = jnp.arange(child_total, dtype=jnp.int32) // block_rows
    row_target, row_global, row_local, row_start, row_counts = child_tables(
        ext_map, rows_grid, front_rows, block_rows
    )
    col_target, _, col_local, _, _ = child_tables(ext_map, groups, front_cols, block_rows)

    own_target = own_slice(row_target, side, row_pos * block_rows, block_rows)
    own_local = own_slice(row_local, side, row_pos * block_rows, block_rows)
    own_global = own_slice(row_global, side, row_pos * block_rows, block_rows)
    own_slot = (own_target ^ row_pos) * cap_rows + own_local // CHUNKS
    row_hot = [
        hot(rows_grid * cap_rows, jnp.where(own_global % CHUNKS == part, own_slot, -1))
        for part in range(CHUNKS)
    ]

    from_row = jnp.arange(rows_grid, dtype=jnp.int32)[:, None] ^ row_pos
    chosen = from_row == jnp.arange(rows_grid, dtype=jnp.int32)[None, :]

    def arriving(table):
        table = lax.dynamic_index_in_dim(table, side, 0, keepdims=False)
        table = lax.dynamic_slice_in_dim(table, row_pos, 1, 1)[:, 0]
        return jnp.sum(jnp.where(chosen, table[None, :], 0), axis=1)[:, None]

    start_here = arriving(row_start)
    count_here = arriving(row_counts)
    slot_ids = jnp.arange(cap_rows, dtype=jnp.int32)[None, :] * CHUNKS
    pack_hot = []
    for part in range(CHUNKS):
        inner = slot_ids + (part - start_here) % CHUNKS
        packed = jnp.where(inner < count_here, (start_here + inner) // CHUNKS, -1)
        pack_hot.append(hot(held_count, packed.reshape(-1)))

    own_cext = own_slice(ext_map, side, col_pos * block_rows, block_rows)
    own_ctarget = own_slice(col_target, side, col_pos * block_rows, block_rows)
    own_crank = own_slice(col_local, side, col_pos * block_rows, block_rows)
    col_hot = hot(groups * cap_cols, own_ctarget * cap_cols + own_crank)

    def exchange(sent):
        blocks = [sent[:cap_rows]]
        for offset in range(1, rows_grid):
            pairs = [(here, here ^ offset) for here in range(rows_grid)]
            block = sent[offset * cap_rows : (offset + 1) * cap_rows]
            blocks.append(lax.ppermute(block, "row", pairs))
        return jnp.concatenate(blocks, axis=0)

    landed = []
    for part in range(CHUNKS):
        sent = dot(row_hot[part], update, PLAIN).astype(jnp.bfloat16)
        arrived = exchange(sent)
        held = dot(pack_hot[part], arrived, PLAIN).astype(jnp.bfloat16)
        send_cols = dot(col_hot, held, LAST).astype(jnp.bfloat16)
        got = lax.all_to_all(
            send_cols.reshape(groups, cap_cols, held_count),
            ("sib", "col"),
            split_axis=0,
            concat_axis=0,
            tiled=True,
        )
        landed.append(got.reshape(2, cols_grid * cap_cols, held_count))

    row_place = []
    col_place = []
    for sibling in range(2):
        here = row_target[sibling] == row_pos
        order = (row_global[sibling] % CHUNKS) * held_count + row_global[sibling] // CHUNKS
        row_place.append(
            at_place(
                block_rows,
                jnp.where(here, order, -1),
                ext_map[sibling] - row_pos * front_rows,
            )
        )
        here = col_target[sibling] == group_pos
        col_place.append(
            at_place(
                cols_grid * cap_cols,
                jnp.where(here, block_ids * cap_cols + col_local[sibling], -1),
                ext_map[sibling] - group_pos * front_cols,
            )
        )

    strip = dot(update, hot(wide, own_cext), LAST).astype(jnp.bfloat16)
    strip = lax.psum(strip, "col")
    strips = []
    for part in range(CHUNKS):
        sent = dot(row_hot[part], strip, PLAIN).astype(jnp.bfloat16)
        strips.append(dot(pack_hot[part], exchange(sent), PLAIN).astype(jnp.bfloat16))
    strip = jnp.concatenate(strips, axis=0)
    other = lax.ppermute(strip, "sib", [(0, 1), (1, 0)])
    own_rows = hot(front_rows, jnp.where(side == 0, row_place[0], row_place[1]))
    other_rows = hot(front_rows, jnp.where(side == 0, row_place[1], row_place[0]))
    panels = dot(own_rows, strip, PLAIN) + dot(other_rows, other, PLAIN)

    factors = []
    for step in range(NPANEL):
        column = panels[:, step * PANEL : (step + 1) * PANEL]
        for earlier, factor in enumerate(factors):
            first = step * PANEL
            top = lax.slice_in_dim(factor, first % front_rows, first % front_rows + PANEL, axis=0)
            top = broadcast(top, "row", first // front_rows)
            column = column - dot(factor, top, LAST)
        factors.append(dot(column.astype(jnp.bfloat16), diag_inverse[step], LAST).astype(jnp.bfloat16))
    factor = jnp.concatenate(factors, axis=1)
    root_row = group_pos * front_cols // front_rows
    start_row = group_pos * front_cols % front_rows
    across = broadcast(lax.dynamic_slice_in_dim(factor, start_row, front_cols, 0), "row", root_row)

    col_pick = [hot(front_cols, place) for place in col_place]
    front_block = -dot(factor, across, LAST)
    for part in range(CHUNKS):
        spread = jnp.concatenate(
            [dot(landed[part][s], col_pick[s], (((0,), (1,)), ((), ()))).astype(jnp.bfloat16) for s in range(2)],
            axis=0,
        )
        places = jnp.concatenate(
            [row_place[s][part * held_count : (part + 1) * held_count] for s in range(2)]
        )
        front_block = front_block + dot(hot(front_rows, places), spread, PLAIN)
    return front_block.astype(jnp.bfloat16), factor


def solution(mesh):
    placed = (P("sib", "row", "col"), P(), P())
    return jax.shard_map(
        on_device,
        mesh=mesh,
        in_specs=placed,
        out_specs=(P("row", ("sib", "col")), P("row", None)),
        check_vma=False,
    )
```

```python
import jax
import jax.numpy as jnp
from jax import lax
from jax.sharding import PartitionSpec as P

FRONT = 16384
PANEL = 256
NPANEL = 2


def broadcast(shard, axis, root):
    mine = lax.axis_index(axis) == root
    return lax.psum(jnp.where(mine, shard, jnp.zeros_like(shard)), axis)


CHUNKS = 2
LAST = (((1,), (1,)), ((), ()))
PLAIN = (((1,), (0,)), ((), ()))


def dot(a, b, dims):
    return lax.dot_general(a, b, dims, preferred_element_type=jnp.float32)


def child_tables(ext_map, part_count, stride, block_rows):
    target = ext_map // stride
    part_ids = jnp.arange(part_count, dtype=jnp.int32)
    onehot = (target[:, :, None] == part_ids[None, None, :]).astype(jnp.int32)
    before = jnp.cumsum(onehot, axis=1) - onehot
    global_rank = jnp.sum(before * onehot, axis=2)
    block_start = before[:, ::block_rows, :]
    starts = jnp.repeat(block_start, block_rows, axis=1)
    local_rank = global_rank - jnp.sum(starts * onehot, axis=2)
    counts = jnp.sum(onehot.reshape(2, -1, block_rows, part_count), axis=2)
    return target, global_rank, local_rank, block_start, counts


def own_slice(table, side_index, first_row, block_rows):
    picked = lax.dynamic_index_in_dim(table, side_index, 0, keepdims=False)
    return lax.dynamic_slice_in_dim(picked, first_row, block_rows, 0)


def at_place(count, place, value):
    here = jnp.arange(count, dtype=jnp.int32)[:, None] == place[None, :]
    return jnp.sum(jnp.where(here, value[None, :] + 1, 0), axis=1) - 1


def hot(count, index):
    return (jnp.arange(count, dtype=jnp.int32)[:, None] == index[None, :]).astype(jnp.bfloat16)


def on_device(child_update, ext_map, diag_inverse):
    rows_grid = lax.axis_size("row")
    cols_grid = lax.axis_size("col")
    groups = lax.axis_size("sib") * cols_grid
    side = lax.axis_index("sib")
    row_pos = lax.axis_index("row")
    col_pos = lax.axis_index("col")
    group_pos = side * cols_grid + col_pos
    update = child_update[0]
    block_rows = child_update.shape[1]
    child_total = ext_map.shape[1]
    front_rows = FRONT // rows_grid
    front_cols = FRONT // groups
    mean_load = block_rows // groups
    cap_cols = 2 * mean_load
    cap_rows = 4 * mean_load // CHUNKS
    held_count = block_rows // CHUNKS
    wide = NPANEL * PANEL
    block_ids = jnp.arange(child_total, dtype=jnp.int32) // block_rows
    row_target, row_global, row_local, row_start, row_counts = child_tables(
        ext_map, rows_grid, front_rows, block_rows
    )
    col_target, _, col_local, _, _ = child_tables(ext_map, groups, front_cols, block_rows)

    own_target = own_slice(row_target, side, row_pos * block_rows, block_rows)
    own_local = own_slice(row_local, side, row_pos * block_rows, block_rows)
    own_global = own_slice(row_global, side, row_pos * block_rows, block_rows)
    own_slot = (own_target ^ row_pos) * cap_rows + own_local // CHUNKS
    row_hot = [
        hot(rows_grid * cap_rows, jnp.where(own_global % CHUNKS == part, own_slot, -1))
        for part in range(CHUNKS)
    ]

    from_row = jnp.arange(rows_grid, dtype=jnp.int32)[:, None] ^ row_pos
    chosen = from_row == jnp.arange(rows_grid, dtype=jnp.int32)[None, :]

    def arriving(table):
        table = lax.dynamic_index_in_dim(table, side, 0, keepdims=False)
        table = lax.dynamic_slice_in_dim(table, row_pos, 1, 1)[:, 0]
        return jnp.sum(jnp.where(chosen, table[None, :], 0), axis=1)[:, None]

    start_here = arriving(row_start)
    count_here = arriving(row_counts)
    slot_ids = jnp.arange(cap_rows, dtype=jnp.int32)[None, :] * CHUNKS
    pack_hot = []
    for part in range(CHUNKS):
        inner = slot_ids + (part - start_here) % CHUNKS
        packed = jnp.where(inner < count_here, (start_here + inner) // CHUNKS, -1)
        pack_hot.append(hot(held_count, packed.reshape(-1)))

    own_cext = own_slice(ext_map, side, col_pos * block_rows, block_rows)
    own_ctarget = own_slice(col_target, side, col_pos * block_rows, block_rows)
    own_crank = own_slice(col_local, side, col_pos * block_rows, block_rows)
    col_hot = hot(groups * cap_cols, own_ctarget * cap_cols + own_crank)

    def exchange(sent):
        blocks = [sent[:cap_rows]]
        for offset in range(1, rows_grid):
            pairs = [(here, here ^ offset) for here in range(rows_grid)]
            block = sent[offset * cap_rows : (offset + 1) * cap_rows]
            blocks.append(lax.ppermute(block, "row", pairs))
        return jnp.concatenate(blocks, axis=0)

    landed = []
    for part in range(CHUNKS):
        sent = dot(row_hot[part], update, PLAIN).astype(jnp.bfloat16)
        arrived = exchange(sent)
        held = dot(pack_hot[part], arrived, PLAIN).astype(jnp.bfloat16)
        send_cols = dot(col_hot, held, LAST).astype(jnp.bfloat16)
        got = lax.all_to_all(
            send_cols.reshape(groups, cap_cols, held_count),
            ("sib", "col"),
            split_axis=0,
            concat_axis=0,
            tiled=True,
        )
        landed.append(got.reshape(2, cols_grid * cap_cols, held_count))

    row_place = []
    col_place = []
    for sibling in range(2):
        here = row_target[sibling] == row_pos
        order = (row_global[sibling] % CHUNKS) * held_count + row_global[sibling] // CHUNKS
        row_place.append(
            at_place(
                block_rows,
                jnp.where(here, order, -1),
                ext_map[sibling] - row_pos * front_rows,
            )
        )
        here = col_target[sibling] == group_pos
        col_place.append(
            at_place(
                cols_grid * cap_cols,
                jnp.where(here, block_ids * cap_cols + col_local[sibling], -1),
                ext_map[sibling] - group_pos * front_cols,
            )
        )

    strip = dot(update, hot(wide, own_cext), LAST).astype(jnp.bfloat16)
    strip = lax.psum(strip, "col")
    own_rext = own_slice(ext_map, side, row_pos * block_rows, block_rows)
    tops = dot(hot(wide, own_rext)[PANEL:], strip[:, : wide - PANEL], PLAIN)
    tops = lax.psum(tops, ("sib", "row"))
    strips = []
    for part in range(CHUNKS):
        sent = dot(row_hot[part], strip, PLAIN).astype(jnp.bfloat16)
        strips.append(dot(pack_hot[part], exchange(sent), PLAIN).astype(jnp.bfloat16))
    strip = jnp.concatenate(strips, axis=0)
    other = lax.ppermute(strip, "sib", [(0, 1), (1, 0)])
    own_rows = hot(front_rows, jnp.where(side == 0, row_place[0], row_place[1]))
    other_rows = hot(front_rows, jnp.where(side == 0, row_place[1], row_place[0]))
    panels = dot(own_rows, strip, PLAIN) + dot(other_rows, other, PLAIN)

    top_factors = []
    for step in range(NPANEL - 1):
        column = tops[:, step * PANEL : (step + 1) * PANEL]
        for factor in top_factors:
            column = column - dot(factor, factor[(step - 1) * PANEL : step * PANEL], LAST)
        top_factors.append(
            dot(column.astype(jnp.bfloat16), diag_inverse[step], LAST).astype(jnp.bfloat16)
        )
    factors = []
    for step in range(NPANEL):
        column = panels[:, step * PANEL : (step + 1) * PANEL]
        for factor, top in zip(factors, top_factors):
            column = column - dot(factor, top[(step - 1) * PANEL : step * PANEL], LAST)
        factors.append(dot(column.astype(jnp.bfloat16), diag_inverse[step], LAST).astype(jnp.bfloat16))
    factor = jnp.concatenate(factors, axis=1)
    root_row = group_pos * front_cols // front_rows
    start_row = group_pos * front_cols % front_rows
    col_pick = [hot(front_cols, place) for place in col_place]

    def placed(part):
        spread = jnp.concatenate(
            [dot(landed[part][s], col_pick[s], (((0,), (1,)), ((), ()))).astype(jnp.bfloat16) for s in range(2)],
            axis=0,
        )
        places = jnp.concatenate(
            [row_place[s][part * held_count : (part + 1) * held_count] for s in range(2)]
        )
        return dot(hot(front_rows, places), spread, PLAIN)

    chosen = lax.dynamic_slice_in_dim(factor, start_row, front_cols, 0)
    across = broadcast(chosen, "row", root_row)
    front_block = placed(0)
    across, front_block = lax.optimization_barrier((across, front_block))
    front_block = front_block - dot(factor, across, LAST)
    landed[1:], front_block = lax.optimization_barrier((landed[1:], front_block))
    for part in range(1, CHUNKS):
        front_block = front_block + placed(part)
    return front_block.astype(jnp.bfloat16), factor


def solution(mesh):
    placed = (P("sib", "row", "col"), P(), P())
    return jax.shard_map(
        on_device,
        mesh=mesh,
        in_specs=placed,
        out_specs=(P("row", ("sib", "col")), P("row", None)),
        check_vma=False,
    )
```

```python
import jax
import jax.numpy as jnp
from jax import lax
from jax.sharding import PartitionSpec as P

FRONT = 16384
PANEL = 256
NPANEL = 2


def broadcast(shard, axis, root):
    mine = lax.axis_index(axis) == root
    return lax.psum(jnp.where(mine, shard, jnp.zeros_like(shard)), axis)


CHUNKS = 4
LAST = (((1,), (1,)), ((), ()))
PLAIN = (((1,), (0,)), ((), ()))


def dot(a, b, dims):
    return lax.dot_general(a, b, dims, preferred_element_type=jnp.float32)


def child_tables(ext_map, part_count, stride, block_rows):
    target = ext_map // stride
    part_ids = jnp.arange(part_count, dtype=jnp.int32)
    onehot = (target[:, :, None] == part_ids[None, None, :]).astype(jnp.int32)
    before = jnp.cumsum(onehot, axis=1) - onehot
    global_rank = jnp.sum(before * onehot, axis=2)
    block_start = before[:, ::block_rows, :]
    starts = jnp.repeat(block_start, block_rows, axis=1)
    local_rank = global_rank - jnp.sum(starts * onehot, axis=2)
    counts = jnp.sum(onehot.reshape(2, -1, block_rows, part_count), axis=2)
    return target, global_rank, local_rank, block_start, counts


def own_slice(table, side_index, first_row, block_rows):
    picked = lax.dynamic_index_in_dim(table, side_index, 0, keepdims=False)
    return lax.dynamic_slice_in_dim(picked, first_row, block_rows, 0)


def at_place(count, place, value):
    here = jnp.arange(count, dtype=jnp.int32)[:, None] == place[None, :]
    return jnp.sum(jnp.where(here, value[None, :] + 1, 0), axis=1) - 1


def hot(count, index):
    return (jnp.arange(count, dtype=jnp.int32)[:, None] == index[None, :]).astype(jnp.bfloat16)


def on_device(child_update, ext_map, diag_inverse):
    rows_grid = lax.axis_size("row")
    cols_grid = lax.axis_size("col")
    groups = lax.axis_size("sib") * cols_grid
    side = lax.axis_index("sib")
    row_pos = lax.axis_index("row")
    col_pos = lax.axis_index("col")
    group_pos = side * cols_grid + col_pos
    update = child_update[0]
    block_rows = child_update.shape[1]
    child_total = ext_map.shape[1]
    front_rows = FRONT // rows_grid
    front_cols = FRONT // groups
    mean_load = block_rows // groups
    cap_cols = 2 * mean_load
    cap_rows = 4 * mean_load // CHUNKS
    held_count = block_rows // CHUNKS
    wide = NPANEL * PANEL
    block_ids = jnp.arange(child_total, dtype=jnp.int32) // block_rows
    row_target, row_global, row_local, row_start, row_counts = child_tables(
        ext_map, rows_grid, front_rows, block_rows
    )
    col_target, _, col_local, _, _ = child_tables(ext_map, groups, front_cols, block_rows)

    own_target = own_slice(row_target, side, row_pos * block_rows, block_rows)
    own_local = own_slice(row_local, side, row_pos * block_rows, block_rows)
    own_global = own_slice(row_global, side, row_pos * block_rows, block_rows)
    own_slot = (own_target ^ row_pos) * cap_rows + own_local // CHUNKS
    row_hot = [
        hot(rows_grid * cap_rows, jnp.where(own_global % CHUNKS == part, own_slot, -1))
        for part in range(CHUNKS)
    ]

    from_row = jnp.arange(rows_grid, dtype=jnp.int32)[:, None] ^ row_pos
    chosen = from_row == jnp.arange(rows_grid, dtype=jnp.int32)[None, :]

    def arriving(table):
        table = lax.dynamic_index_in_dim(table, side, 0, keepdims=False)
        table = lax.dynamic_slice_in_dim(table, row_pos, 1, 1)[:, 0]
        return jnp.sum(jnp.where(chosen, table[None, :], 0), axis=1)[:, None]

    start_here = arriving(row_start)
    count_here = arriving(row_counts)
    slot_ids = jnp.arange(cap_rows, dtype=jnp.int32)[None, :] * CHUNKS
    pack_hot = []
    for part in range(CHUNKS):
        inner = slot_ids + (part - start_here) % CHUNKS
        packed = jnp.where(inner < count_here, (start_here + inner) // CHUNKS, -1)
        pack_hot.append(hot(held_count, packed.reshape(-1)))

    own_cext = own_slice(ext_map, side, col_pos * block_rows, block_rows)
    own_ctarget = own_slice(col_target, side, col_pos * block_rows, block_rows)
    own_crank = own_slice(col_local, side, col_pos * block_rows, block_rows)
    col_hot = hot(groups * cap_cols, own_ctarget * cap_cols + own_crank)

    def exchange(sent):
        blocks = [sent[:cap_rows]]
        for offset in range(1, rows_grid):
            pairs = [(here, here ^ offset) for here in range(rows_grid)]
            block = sent[offset * cap_rows : (offset + 1) * cap_rows]
            blocks.append(lax.ppermute(block, "row", pairs))
        return jnp.concatenate(blocks, axis=0)

    landed = []
    for part in range(CHUNKS):
        sent = dot(row_hot[part], update, PLAIN).astype(jnp.bfloat16)
        arrived = exchange(sent)
        held = dot(pack_hot[part], arrived, PLAIN).astype(jnp.bfloat16)
        send_cols = dot(col_hot, held, LAST).astype(jnp.bfloat16)
        got = lax.all_to_all(
            send_cols.reshape(groups, cap_cols, held_count),
            ("sib", "col"),
            split_axis=0,
            concat_axis=0,
            tiled=True,
        )
        landed.append(got.reshape(2, cols_grid * cap_cols, held_count))

    row_place = []
    col_place = []
    for sibling in range(2):
        here = row_target[sibling] == row_pos
        order = (row_global[sibling] % CHUNKS) * held_count + row_global[sibling] // CHUNKS
        row_place.append(
            at_place(
                block_rows,
                jnp.where(here, order, -1),
                ext_map[sibling] - row_pos * front_rows,
            )
        )
        here = col_target[sibling] == group_pos
        col_place.append(
            at_place(
                cols_grid * cap_cols,
                jnp.where(here, block_ids * cap_cols + col_local[sibling], -1),
                ext_map[sibling] - group_pos * front_cols,
            )
        )

    strip = dot(update, hot(wide, own_cext), LAST).astype(jnp.bfloat16)
    strip = lax.psum(strip, "col")
    own_rext = own_slice(ext_map, side, row_pos * block_rows, block_rows)
    tops = dot(hot(wide, own_rext)[PANEL:], strip[:, : wide - PANEL], PLAIN)
    tops = lax.psum(tops, ("sib", "row"))
    strips = []
    for part in range(CHUNKS):
        sent = dot(row_hot[part], strip, PLAIN).astype(jnp.bfloat16)
        strips.append(dot(pack_hot[part], exchange(sent), PLAIN).astype(jnp.bfloat16))
    strip = jnp.concatenate(strips, axis=0)
    other = lax.ppermute(strip, "sib", [(0, 1), (1, 0)])
    own_rows = hot(front_rows, jnp.where(side == 0, row_place[0], row_place[1]))
    other_rows = hot(front_rows, jnp.where(side == 0, row_place[1], row_place[0]))
    panels = dot(own_rows, strip, PLAIN) + dot(other_rows, other, PLAIN)

    top_factors = []
    for step in range(NPANEL - 1):
        column = tops[:, step * PANEL : (step + 1) * PANEL]
        for factor in top_factors:
            column = column - dot(factor, factor[(step - 1) * PANEL : step * PANEL], LAST)
        top_factors.append(
            dot(column.astype(jnp.bfloat16), diag_inverse[step], LAST).astype(jnp.bfloat16)
        )
    factors = []
    for step in range(NPANEL):
        column = panels[:, step * PANEL : (step + 1) * PANEL]
        for factor, top in zip(factors, top_factors):
            column = column - dot(factor, top[(step - 1) * PANEL : step * PANEL], LAST)
        factors.append(dot(column.astype(jnp.bfloat16), diag_inverse[step], LAST).astype(jnp.bfloat16))
    factor = jnp.concatenate(factors, axis=1)
    root_row = group_pos * front_cols // front_rows
    start_row = group_pos * front_cols % front_rows
    col_pick = [hot(front_cols, place) for place in col_place]

    def placed(part):
        spread = jnp.concatenate(
            [dot(landed[part][s], col_pick[s], (((0,), (1,)), ((), ()))).astype(jnp.bfloat16) for s in range(2)],
            axis=0,
        )
        places = jnp.concatenate(
            [row_place[s][part * held_count : (part + 1) * held_count] for s in range(2)]
        )
        return dot(hot(front_rows, places), spread, PLAIN)

    chosen = lax.dynamic_slice_in_dim(factor, start_row, front_cols, 0)
    across = broadcast(chosen, "row", root_row)
    front_block = placed(0)
    across, front_block = lax.optimization_barrier((across, front_block))
    front_block = front_block - dot(factor, across, LAST)
    for part in range(1, CHUNKS):
        landed[part], front_block = lax.optimization_barrier((landed[part], front_block))
        front_block = front_block + placed(part)
    return front_block.astype(jnp.bfloat16), factor


def solution(mesh):
    placed = (P("sib", "row", "col"), P(), P())
    return jax.shard_map(
        on_device,
        mesh=mesh,
        in_specs=placed,
        out_specs=(P("row", ("sib", "col")), P("row", None)),
        check_vma=False,
    )
```
